128 devices in a mesh: span: 8 (over z_lo, x), seq: 16 (over y, z_hi, core).
Axes of the slice: x: 4, y: 4, z: 4 (z_hi: 2, z_lo: 2; z = z_hi * 2 + z_lo), core: 2. Of those that a mesh axis runs over, the one named last changes fastest.
Arguments:
- queries: bfloat16 [16384, 4096], P(('span', 'seq')), may hold values from -120 to 120
- keys: bfloat16 [16384, 4096], P(('span', 'seq')), may hold values from -6 to 6
- values: bfloat16 [16384, 4096], P(('span', 'seq')), may hold values from -6 to 6
- out_grad: bfloat16 [16384, 4096], P(('span', 'seq')), may hold values from -6 to 6
- block_table: int32 [8, 8], replicated, may hold values from 0 to 1, as said below
Outputs:
- attended: bfloat16 [16384, 4096], P(('span', 'seq'))
- query_grad: bfloat16 [16384, 4096], P(('span', 'seq'))
- key_grad: bfloat16 [16384, 4096], P(('span', 'seq'))
- value_grad: bfloat16 [16384, 4096], P(('span', 'seq'))
The draws below stay inside these ranges and needn't reach their ends.
Inputs may be any that keep to these rules, and one draw needn't show every extreme that they name: block_table[c, c] = 1; the other ones of row c stand only at columns c - 1 and c - 2; span 1 attends span 0, and span 2 attends span 0.
All inputs are finite; a program needn't handle non-finite values.
Results may differ from the reference program's by a relative error of at most 0.0051.
Values may be sent and summed in bfloat16 or wider, within the bound.
No kernel may reach another device: no remote copies, remote signals or barrier semaphores. Data moves between devices by JAX's collectives and lax.ppermute only.
A program may use at most 128 MiB of HBM per device.

```python
import math
import jax
import jax.numpy as jnp
from jax import lax

HEADS = 32
DH = 128
TOK_DEV = 128
SPANS = 8
TOKENS = 16384
HD = 4096
N_SEQ = 16


def shared_keys(key):
    return jnp.clip(jax.random.normal(key, (TOKENS, HD), jnp.float32), -6.0, 6.0)


def draw_keys(key, part):
    base = shared_keys(key)
    return base.astype(jnp.bfloat16)


def draw_queries(key, part):
    key = jax.random.fold_in(key, 5)
    fresh = jnp.clip(jax.random.normal(key, (TOKENS, HD), jnp.float32), -6.0, 6.0)
    return fresh.astype(jnp.bfloat16)


def draw_block_table(key, part):
    key = jax.random.fold_in(key, 23)
    near_key = jax.random.fold_in(key, 1)
    far_key = jax.random.fold_in(key, 2)
    span_ids = jnp.arange(SPANS, dtype=jnp.int32)
    near_bit = jax.random.randint(near_key, (SPANS,), 0, 2).astype(jnp.int32)
    far_bit = jax.random.randint(far_key, (SPANS,), 0, 2).astype(jnp.int32)
    near_bit = jnp.where(span_ids == 1, 1, near_bit)
    far_bit = jnp.where(span_ids == 2, 1, far_bit)
    near_bit = jnp.where(span_ids >= 1, near_bit, 0)
    far_bit = jnp.where(span_ids >= 2, far_bit, 0)
    columns = jnp.arange(SPANS, dtype=jnp.int32)
    own = columns[None, :] == span_ids[:, None]
    near_cell = (near_bit[:, None] > 0) & (columns[None, :] == span_ids[:, None] - 1)
    far_cell = (far_bit[:, None] > 0) & (columns[None, :] == span_ids[:, None] - 2)
    return (own | near_cell | far_cell).astype(jnp.int32)


def block_levels(rng, extent, cuts, smallest, high):
    factor_of = 1.0
    for position, blocks in cuts:
        draws = jax.random.uniform(jax.random.fold_in(jax.random.fold_in(rng, 6), position), (blocks,), jnp.float32, smallest / len(cuts), high / len(cuts))
        factor_of = factor_of * jnp.repeat(jnp.exp(draws), extent[position] // blocks).reshape((-1,) + (1,) * (len(extent) - 1 - position))
    return factor_of


def normal_values(key, dims, spread, bound, pieces=(), kind=jnp.bfloat16):
    array = jax.random.normal(key, dims, jnp.float32) * spread
    if len(pieces) > 0:
        array = block_levels(key, dims, pieces, -0.22, 0.18) * array
    return jnp.clip(array, min=-bound, max=bound).astype(kind)


def setup_inputs(seed: int = 0) -> dict:
    key_list = jax.random.split(jax.random.key(seed), 6)
    queries = draw_queries(jax.random.fold_in(key_list[5], 71), 0)
    keys = draw_keys(jax.random.fold_in(key_list[5], 71), 0)
    values = normal_values(key_list[2], (TOKENS, HD), 1.0, 6.0, ((0, 128),))
    out_grad = normal_values(key_list[3], (TOKENS, HD), 1.0, 6.0, ((0, 128),))
    block_table = draw_block_table(jax.random.fold_in(key_list[5], 71), 0)
    return dict(queries=queries, keys=keys, values=values, out_grad=out_grad, block_table=block_table)


def head_pass(qh, kh, vh, gh, near_k, near_v, far_k, far_v, has_near, has_far):
    scale = 1.0 / math.sqrt(qh.shape[1])
    s_own = jnp.dot(qh, kh.T, preferred_element_type=jnp.float32) * scale
    s_near = jnp.dot(qh, near_k.T, preferred_element_type=jnp.float32) * scale
    s_near = jnp.where(has_near, s_near, jnp.float32(-1e+30))
    s_far = jnp.dot(qh, far_k.T, preferred_element_type=jnp.float32) * scale
    s_far = jnp.where(has_far, s_far, jnp.float32(-1e+30))
    top = jnp.maximum(jnp.maximum(lax.optimization_barrier(jnp.max(s_own, -1)), lax.optimization_barrier(jnp.max(s_near, -1))), lax.optimization_barrier(jnp.max(s_far, -1)))
    e_own = jnp.exp(s_own - top[:, None])
    e_near = jnp.exp(s_near - top[:, None])
    e_far = jnp.exp(s_far - top[:, None])
    total = lax.optimization_barrier(jnp.sum(e_own, -1)) + lax.optimization_barrier(jnp.sum(e_near, -1)) + lax.optimization_barrier(jnp.sum(e_far, -1))
    p_own = e_own / total[:, None]
    p_near = e_near / total[:, None]
    p_far = e_far / total[:, None]
    pb_own = p_own.astype(jnp.bfloat16)
    pb_near = p_near.astype(jnp.bfloat16)
    pb_far = p_far.astype(jnp.bfloat16)
    attended = (jnp.dot(pb_own, vh, preferred_element_type=jnp.float32) + jnp.dot(pb_near, near_v, preferred_element_type=jnp.float32) + jnp.dot(pb_far, far_v, preferred_element_type=jnp.float32)).astype(jnp.bfloat16)
    dp_own = jnp.dot(gh, vh.T, preferred_element_type=jnp.float32)
    dp_near = jnp.dot(gh, near_v.T, preferred_element_type=jnp.float32)
    dp_far = jnp.dot(gh, far_v.T, preferred_element_type=jnp.float32)
    delta = lax.optimization_barrier(jnp.sum(p_own * dp_own, -1)) + lax.optimization_barrier(jnp.sum(p_near * dp_near, -1)) + lax.optimization_barrier(jnp.sum(p_far * dp_far, -1))
    ds_own = (p_own * (dp_own - delta[:, None]) * scale).astype(jnp.bfloat16)
    ds_near = (p_near * (dp_near - delta[:, None]) * scale).astype(jnp.bfloat16)
    ds_far = (p_far * (dp_far - delta[:, None]) * scale).astype(jnp.bfloat16)
    query_grad = (jnp.dot(ds_own, kh, preferred_element_type=jnp.float32) + jnp.dot(ds_near, near_k, preferred_element_type=jnp.float32) + jnp.dot(ds_far, far_k, preferred_element_type=jnp.float32)).astype(jnp.bfloat16)
    key_grad = jnp.dot(ds_own.T, qh, preferred_element_type=jnp.float32).astype(jnp.bfloat16)
    value_grad = jnp.dot(pb_own.T, gh, preferred_element_type=jnp.float32).astype(jnp.bfloat16)
    return (attended, query_grad, key_grad, value_grad)

def reference(queries, keys, values, out_grad, block_table):
    width = TOK_DEV * N_SEQ
    half = width // 2
    q_all = queries.reshape(SPANS, width, HEADS, DH)
    k_all = keys.reshape(SPANS, width, HEADS, DH)
    v_all = values.reshape(SPANS, width, HEADS, DH)
    g_all = out_grad.reshape(SPANS, width, HEADS, DH)

    def single(index):
        span_pos = index // HEADS
        head_pos = index % HEADS
        near_src = jnp.maximum(span_pos - 1, 0).astype(jnp.int32)
        far_src = jnp.maximum(span_pos - 2, 0).astype(jnp.int32)
        has_near = jnp.where(span_pos >= 1, block_table[span_pos, near_src], 0) > 0
        has_far = jnp.where(span_pos >= 2, block_table[span_pos, far_src], 0) > 0
        return head_pass(q_all[span_pos, :, head_pos, :], k_all[span_pos, :, head_pos, :], v_all[span_pos, :, head_pos, :], g_all[span_pos, :, head_pos, :], k_all[near_src, half:, head_pos, :], v_all[near_src, half:, head_pos, :], k_all[far_src, half:, head_pos, :], v_all[far_src, half:, head_pos, :], has_near, has_far)
    results = lax.map(single, jnp.arange(SPANS * HEADS, dtype=jnp.int32))

    def arrange(stacked):
        return stacked.reshape(SPANS, HEADS, width, DH).transpose(0, 2, 1, 3).reshape(TOKENS, HD)
    return (arrange(results[0]), arrange(results[1]), arrange(results[2]), arrange(results[3]))
```

```python
import functools
import math

import jax
import jax.numpy as jnp
from jax import lax
from jax.experimental import pallas as pl
from jax.experimental.pallas import tpu as pltpu
from jax.sharding import PartitionSpec as P

DH = 128
F32 = jnp.float32
BF16 = jnp.bfloat16
SCALE = 1.0 / math.sqrt(DH)
SCALE2 = SCALE * math.log2(math.e)
NT = (((1,), (1,)), ((), ()))
NN = (((1,), (0,)), ((), ()))
TN = (((0,), (0,)), ((), ()))
VMEM_LIMIT = 56 * 2**20


def dot(a, b, dims):
    return lax.dot_general(a, b, dims, preferred_element_type=F32)


def fold(op, x):
    result = x[:, :DH]
    for i in range(DH, x.shape[1], DH):
        result = op(result, x[:, i : i + DH])
    return result


def attention_kernel(
    q_rows, k_cols, flags_ref, x_ref, near_ref, far_ref, out_ref, k_s, v_s, s_s, dp_s, dk_s, dv_s
):
    rows = x_ref.shape[0] * DH
    half = near_ref.shape[0] * DH
    near, far = flags_ref[0], flags_ref[1]
    k_s[:rows] = x_ref[:, 0].reshape(rows, DH)
    v_s[:rows] = x_ref[:, 1].reshape(rows, DH)

    @pl.when(near > 0)
    def _():
        k_s[rows : rows + half] = near_ref[:, 0].reshape(half, DH)
        v_s[rows : rows + half] = near_ref[:, 1].reshape(half, DH)

    @pl.when(far > 0)
    def _():
        start = pl.multiple_of(rows + near * half, half)
        k_s[pl.ds(start, half)] = far_ref[:, 0].reshape(half, DH)
        v_s[pl.ds(start, half)] = far_ref[:, 1].reshape(half, DH)

    dk_s[...] = jnp.zeros_like(dk_s)
    dv_s[...] = jnp.zeros_like(dv_s)
    group = q_rows // DH

    def run(contexts):
        chunks = range(0, rows + contexts * half, k_cols)

        def block(i, carry):
            here = pl.ds(i * group, group)
            q = x_ref[here, 2].reshape(q_rows, DH)
            g = x_ref[here, 3].reshape(q_rows, DH)
            top = None
            for c in chunks:
                s = dot(q, k_s[c : c + k_cols], NT)
                s_s[:, c : c + k_cols] = s
                part = fold(jnp.maximum, s)
                top = part if top is None else jnp.maximum(top, part)
            top = jnp.max(top, 1, keepdims=True) * SCALE2
            total = delta = out = None
            for c in chunks:
                e = jnp.exp2(s_s[:, c : c + k_cols] * SCALE2 - top)
                s_s[:, c : c + k_cols] = e
                dp = dot(g, v_s[c : c + k_cols], NT)
                dp_s[:, c : c + k_cols] = dp
                t_part, d_part = fold(jnp.add, e), fold(jnp.add, e * dp)
                o_part = dot(e.astype(BF16), v_s[c : c + k_cols], NN)
                total = t_part if total is None else total + t_part
                delta = d_part if delta is None else delta + d_part
                out = o_part if out is None else out + o_part
            inv = 1.0 / jnp.sum(total, 1, keepdims=True)
            delta = jnp.sum(delta, 1, keepdims=True) * inv
            out_ref[here, 0] = (out * inv).astype(BF16).reshape(group, DH, DH)
            g_over = (g.astype(F32) * inv).astype(BF16)
            q_over = (q.astype(F32) * (inv * SCALE)).astype(BF16)
            dq = None
            for c in chunks:
                e = s_s[:, c : c + k_cols]
                ds = (e * (dp_s[:, c : c + k_cols] - delta)).astype(BF16)
                part = dot(ds, k_s[c : c + k_cols], NN)
                dq = part if dq is None else dq + part
                if c < rows:
                    dk_s[c : c + k_cols] += dot(ds, q_over, TN)
                    dv_s[c : c + k_cols] += dot(e.astype(BF16), g_over, TN)
            out_ref[here, 1] = (dq * (inv * SCALE)).astype(BF16).reshape(group, DH, DH)
            return carry

        lax.fori_loop(0, rows // q_rows, block, 0)

    for contexts in range(3):
        pl.when(near + far == contexts)(functools.partial(run, contexts))
    out_ref[:, 2] = dk_s[...].astype(BF16).reshape(rows // DH, DH, DH)
    out_ref[:, 3] = dv_s[...].astype(BF16).reshape(rows // DH, DH, DH)


def attention(flags, x, near, far, q_rows=256, k_cols=1024):
    rows, half = x.shape[0] * DH, near.shape[0] * DH
    length = rows + 2 * half
    vmem = pl.BlockSpec(memory_space=pltpu.VMEM)
    return pl.pallas_call(
        functools.partial(attention_kernel, q_rows, k_cols),
        out_shape=jax.ShapeDtypeStruct(x.shape, BF16),
        in_specs=[pl.BlockSpec(memory_space=pltpu.SMEM), vmem, vmem, vmem],
        out_specs=vmem,
        scratch_shapes=[
            pltpu.VMEM((length, DH), BF16),
            pltpu.VMEM((length, DH), BF16),
            pltpu.VMEM((q_rows, length), F32),
            pltpu.VMEM((q_rows, length), F32),
            pltpu.VMEM((rows, DH), F32),
            pltpu.VMEM((rows, DH), F32),
        ],
        compiler_params=pltpu.CompilerParams(vmem_limit_bytes=VMEM_LIMIT),
        cost_estimate=pl.CostEstimate(
            flops=40 * 10**9, bytes_accessed=6 * 2**20, transcendentals=rows * length
        ),
        name="attention",
    )(flags, x, near, far)


def pack_kernel(k_ref, v_ref, q_ref, g_ref, a_ref, b_ref):
    for j in range(a_ref.shape[0]):
        for i, ref in enumerate((k_ref, v_ref, q_ref, g_ref)):
            a_ref[j, i] = ref[:, 2 * j * DH : (2 * j + 1) * DH]
            b_ref[j, i] = ref[:, (2 * j + 1) * DH : (2 * j + 2) * DH]


def pack(arrays):
    tokens, width = arrays[0].shape
    dests = width // (2 * DH)
    step = 4
    shape = jax.ShapeDtypeStruct((dests, 4, tokens, DH), BF16)
    return pl.pallas_call(
        pack_kernel,
        grid=(dests // step,),
        out_shape=(shape, shape),
        in_specs=[pl.BlockSpec((tokens, step * 2 * DH), lambda j: (0, j))] * 4,
        out_specs=[pl.BlockSpec((step, 4, tokens, DH), lambda j: (j, 0, 0, 0))] * 2,
        cost_estimate=pl.CostEstimate(flops=0, bytes_accessed=8 * 2**20, transcendentals=0),
        name="pack",
    )(*arrays)


def unpack_kernel(a_ref, b_ref, *out_refs):
    for j in range(a_ref.shape[0]):
        for i, ref in enumerate(out_refs):
            ref[:, 2 * j * DH : (2 * j + 1) * DH] = a_ref[j, i]
            ref[:, (2 * j + 1) * DH : (2 * j + 2) * DH] = b_ref[j, i]


def unpack(a, b):
    sources, _, tokens, _ = a.shape
    step = 4
    shape = jax.ShapeDtypeStruct((tokens, sources * 2 * DH), BF16)
    return pl.pallas_call(
        unpack_kernel,
        grid=(sources // step,),
        out_shape=(shape,) * 4,
        in_specs=[pl.BlockSpec((step, 4, tokens, DH), lambda j: (j, 0, 0, 0))] * 2,
        out_specs=[pl.BlockSpec((tokens, step * 2 * DH), lambda j: (0, j))] * 4,
        cost_estimate=pl.CostEstimate(flops=0, bytes_accessed=8 * 2**20, transcendentals=0),
        name="unpack",
    )(a, b)


def passed_along(block, axis, distance):
    devices = range(lax.axis_size(axis))
    route = [(i - distance, i) for i in devices if i - distance in devices]
    return lax.ppermute(block, axis, route)


def exchange(block):
    return lax.all_to_all(block, "seq", split_axis=0, concat_axis=0, tiled=True)


def body(queries, keys, values, out_grad, block_table):
    span = lax.axis_index("span")
    near = jnp.where(span >= 1, block_table[span, jnp.maximum(span - 1, 0)], 0) > 0
    far = jnp.where(span >= 2, block_table[span, jnp.maximum(span - 2, 0)], 0) > 0
    flags = jnp.stack([near, far]).astype(jnp.int32)
    results = []
    for packed in pack((keys, values, queries, out_grad)):
        x = exchange(packed)
        tail = x[x.shape[0] // 2 :, :2]
        y = attention(flags, x, passed_along(tail, "span", 1), passed_along(tail, "span", 2))
        results.append(exchange(y))
    attended, query_grad, key_grad, value_grad = unpack(*results)
    return (attended, query_grad, key_grad, value_grad)


def solution(mesh):
    rows = P(("span", "seq"), None)
    return jax.shard_map(
        body,
        mesh=mesh,
        in_specs=(rows, rows, rows, rows, P()),
        out_specs=(rows, rows, rows, rows),
        check_vma=False,
    )
```

```python
import functools
import math

import jax
import jax.numpy as jnp
from jax import lax
from jax.experimental import pallas as pl
from jax.experimental.pallas import tpu as pltpu
from jax.sharding import PartitionSpec as P

DH = 128
F32 = jnp.float32
BF16 = jnp.bfloat16
SCALE = 1.0 / math.sqrt(DH)
SCALE2 = SCALE * math.log2(math.e)
NT = (((1,), (1,)), ((), ()))
NN = (((1,), (0,)), ((), ()))
TN = (((0,), (0,)), ((), ()))
VMEM_LIMIT = 56 * 2**20


def dot(a, b, dims):
    return lax.dot_general(a, b, dims, preferred_element_type=F32)


def fold(op, x):
    result = x[:, :DH]
    for i in range(DH, x.shape[1], DH):
        result = op(result, x[:, i : i + DH])
    return result


def attention_kernel(
    q_rows, k_cols, flags_ref, kv_ref, qg_ref, near_ref, far_ref, out_ref, k_s, v_s, s_s, dp_s, dk_s, dv_s
):
    rows = qg_ref.shape[0] * DH
    half = near_ref.shape[0] * DH
    near, far = flags_ref[0], flags_ref[1]
    k_s[:rows] = kv_ref[:, 0, 0].reshape(rows, DH)
    v_s[:rows] = kv_ref[:, 0, 1].reshape(rows, DH)

    @pl.when(near > 0)
    def _():
        k_s[rows : rows + half] = near_ref[:, 0].reshape(half, DH)
        v_s[rows : rows + half] = near_ref[:, 1].reshape(half, DH)

    @pl.when(far > 0)
    def _():
        start = pl.multiple_of(rows + near * half, half)
        k_s[pl.ds(start, half)] = far_ref[:, 0].reshape(half, DH)
        v_s[pl.ds(start, half)] = far_ref[:, 1].reshape(half, DH)

    dk_s[...] = jnp.zeros_like(dk_s)
    dv_s[...] = jnp.zeros_like(dv_s)
    group = q_rows // DH

    def run(contexts):
        chunks = range(0, rows + contexts * half, k_cols)

        def block(i, carry):
            here = pl.ds(i * group, group)
            q = qg_ref[here, 0].reshape(q_rows, DH)
            g = qg_ref[here, 1].reshape(q_rows, DH)
            top = None
            for c in chunks:
                s = dot(q, k_s[c : c + k_cols], NT)
                s_s[:, c : c + k_cols] = s
                part = fold(jnp.maximum, s)
                top = part if top is None else jnp.maximum(top, part)
            top = jnp.max(top, 1, keepdims=True) * SCALE2
            total = delta = out = None
            for c in chunks:
                e = jnp.exp2(s_s[:, c : c + k_cols] * SCALE2 - top)
                s_s[:, c : c + k_cols] = e
                dp = dot(g, v_s[c : c + k_cols], NT)
                dp_s[:, c : c + k_cols] = dp
                t_part, d_part = fold(jnp.add, e), fold(jnp.add, e * dp)
                o_part = dot(e.astype(BF16), v_s[c : c + k_cols], NN)
                total = t_part if total is None else total + t_part
                delta = d_part if delta is None else delta + d_part
                out = o_part if out is None else out + o_part
            inv = 1.0 / jnp.sum(total, 1, keepdims=True)
            delta = jnp.sum(delta, 1, keepdims=True) * inv
            out_ref[here, 0] = (out * inv).astype(BF16).reshape(group, DH, DH)
            g_over = (g.astype(F32) * inv).astype(BF16)
            q_over = (q.astype(F32) * (inv * SCALE)).astype(BF16)
            dq = None
            for c in chunks:
                e = s_s[:, c : c + k_cols]
                ds = (e * (dp_s[:, c : c + k_cols] - delta)).astype(BF16)
                part = dot(ds, k_s[c : c + k_cols], NN)
                dq = part if dq is None else dq + part
                if c < rows:
                    dk_s[c : c + k_cols] += dot(ds, q_over, TN)
                    dv_s[c : c + k_cols] += dot(e.astype(BF16), g_over, TN)
            out_ref[here, 1] = (dq * (inv * SCALE)).astype(BF16).reshape(group, DH, DH)
            return carry

        lax.fori_loop(0, rows // q_rows, block, 0)

    for contexts in range(3):
        pl.when(near + far == contexts)(functools.partial(run, contexts))
    out_ref[:, 2] = dk_s[...].astype(BF16).reshape(rows // DH, DH, DH)
    out_ref[:, 3] = dv_s[...].astype(BF16).reshape(rows // DH, DH, DH)


def attention(flags, unit, kv, qg, near, far, q_rows=256, k_cols=1024):
    sources = qg.shape[0]
    rows, half = sources * DH, near.shape[0] * DH
    length = rows + 2 * half

    def whole(array):
        return pl.BlockSpec(array.shape, lambda i: (0,) * array.ndim)

    out = jax.ShapeDtypeStruct((sources, 4, DH, DH), BF16)
    return pl.pallas_call(
        functools.partial(attention_kernel, q_rows, k_cols),
        grid=(1,),
        out_shape=out,
        in_specs=[
            pl.BlockSpec(memory_space=pltpu.SMEM),
            pl.BlockSpec((sources, 1, 2, DH, DH), lambda i: (0, unit, 0, 0, 0)),
            whole(qg),
            whole(near),
            whole(far),
        ],
        out_specs=whole(out),
        scratch_shapes=[
            pltpu.VMEM((length, DH), BF16),
            pltpu.VMEM((length, DH), BF16),
            pltpu.VMEM((q_rows, length), F32),
            pltpu.VMEM((q_rows, length), F32),
            pltpu.VMEM((rows, DH), F32),
            pltpu.VMEM((rows, DH), F32),
        ],
        compiler_params=pltpu.CompilerParams(vmem_limit_bytes=VMEM_LIMIT),
        cost_estimate=pl.CostEstimate(
            flops=40 * 10**9, bytes_accessed=6 * 2**20, transcendentals=rows * length
        ),
        name="attention",
    )(flags, kv, qg, near, far)


def column(unit, dest, flip):
    pair = dest + flip * (2 - dest % 4 // 2 * 4) if dest % 2 else dest
    return pl.ds(pl.multiple_of((2 * pair + unit) * DH, DH), DH)


def pack_kernel(flip_ref, x_ref, y_ref, a_ref, b_ref):
    for j in range(a_ref.shape[0]):
        for i, ref in enumerate((x_ref, y_ref)):
            a_ref[j, i] = ref[:, column(0, j, flip_ref[0])]
            b_ref[j, i] = ref[:, column(1, j, flip_ref[0])]


def pack_joint_kernel(flip_ref, x_ref, y_ref, out_ref):
    for j in range(out_ref.shape[0]):
        for i, ref in enumerate((x_ref, y_ref)):
            for unit in range(2):
                out_ref[j, unit, i] = ref[:, column(unit, j, flip_ref[0])]


def pack(flip, arrays, joint, step=8):
    tokens, width = arrays[0].shape
    dests = width // (2 * DH)
    if joint:
        kernel, dims, count = pack_joint_kernel, (2, 2, tokens, DH), 1
    else:
        kernel, dims, count = pack_kernel, (2, tokens, DH), 2
    spec = pl.BlockSpec((step, *dims), lambda j: (j,) + (0,) * len(dims))
    columns = pl.BlockSpec((tokens, step * 2 * DH), lambda j: (0, j))
    return pl.pallas_call(
        kernel,
        grid=(dests // step,),
        out_shape=(jax.ShapeDtypeStruct((dests, *dims), BF16),) * count,
        in_specs=[pl.BlockSpec(memory_space=pltpu.SMEM), columns, columns],
        out_specs=[spec] * count,
        compiler_params=pltpu.CompilerParams(vmem_limit_bytes=VMEM_LIMIT),
        cost_estimate=pl.CostEstimate(flops=0, bytes_accessed=4 * 2**20, transcendentals=0),
        name="pack",
    )(flip, *arrays)


def unpack_kernel(flip_ref, a_ref, b_ref, *out_refs):
    for j in range(a_ref.shape[0]):
        for i, ref in enumerate(out_refs):
            ref[:, column(0, j, flip_ref[0])] = a_ref[j, i]
            ref[:, column(1, j, flip_ref[0])] = b_ref[j, i]


def unpack(flip, a, b, step=8):
    sources, _, tokens, _ = a.shape
    shape = jax.ShapeDtypeStruct((tokens, sources * 2 * DH), BF16)
    return pl.pallas_call(
        unpack_kernel,
        grid=(sources // step,),
        out_shape=(shape,) * 4,
        in_specs=[pl.BlockSpec(memory_space=pltpu.SMEM)]
        + [pl.BlockSpec((step, 4, tokens, DH), lambda j: (j, 0, 0, 0))] * 2,
        out_specs=[pl.BlockSpec((tokens, step * 2 * DH), lambda j: (0, j))] * 4,
        compiler_params=pltpu.CompilerParams(vmem_limit_bytes=VMEM_LIMIT),
        cost_estimate=pl.CostEstimate(flops=0, bytes_accessed=8 * 2**20, transcendentals=0),
        name="unpack",
    )(flip, a, b)


def passed_along(block, distance):
    spans, width = lax.axis_size("span"), lax.axis_size("seq")
    route = []
    for c in range(spans - distance):
        crosses = (c < spans // 2) != (c + distance < spans // 2)
        for j in range(width):
            to = j ^ 2 if crosses and j % 2 else j
            route.append((c * width + j, (c + distance) * width + to))
    return lax.ppermute(block, ("span", "seq"), route)


def exchange(block):
    return lax.all_to_all(block, "seq", split_axis=0, concat_axis=0, tiled=True)


def body(queries, keys, values, out_grad, block_table):
    span = lax.axis_index("span")
    near = jnp.where(span >= 1, block_table[span, jnp.maximum(span - 1, 0)], 0) > 0
    far = jnp.where(span >= 2, block_table[span, jnp.maximum(span - 2, 0)], 0) > 0
    flags = jnp.stack([near, far]).astype(jnp.int32)
    flip = (span >= lax.axis_size("span") // 2).astype(jnp.int32)[None]
    kv = exchange(pack(flip, (keys, values), True)[0])
    packed = pack(flip, (queries, out_grad), False)
    tails = [kv[kv.shape[0] // 2 :, unit] for unit in range(2)]
    contexts = [(passed_along(t, 1), passed_along(t, 2)) for t in tails]
    results = []
    for unit in range(2):
        y = attention(flags, unit, kv, exchange(packed[unit]), *contexts[unit])
        results.append(exchange(y))
    attended, query_grad, key_grad, value_grad = unpack(flip, *results)
    return (attended, query_grad, key_grad, value_grad)


def solution(mesh):
    rows = P(("span", "seq"), None)
    return jax.shard_map(
        body,
        mesh=mesh,
        in_specs=(rows, rows, rows, rows, P()),
        out_specs=(rows, rows, rows, rows),
        check_vma=False,
    )
```

```python
import functools
import math

import jax
import jax.numpy as jnp
from jax import lax
from jax.experimental import pallas as pl
from jax.experimental.pallas import tpu as pltpu
from jax.sharding import PartitionSpec as P

DH = 128
F32 = jnp.float32
BF16 = jnp.bfloat16
SCALE = 1.0 / math.sqrt(DH)
SCALE2 = SCALE * math.log2(math.e)
NT = (((1,), (1,)), ((), ()))
NN = (((1,), (0,)), ((), ()))
TN = (((0,), (0,)), ((), ()))
ATTENTION_VMEM = 50 * 2**20
COPY_VMEM = 16 * 2**20


def dot(a, b, dims):
    return lax.dot_general(a, b, dims, preferred_element_type=F32)


def fold(op, x):
    result = x[:, :DH]
    for i in range(DH, x.shape[1], DH):
        result = op(result, x[:, i : i + DH])
    return result


def attention_kernel(
    q_rows, k_cols, unit, flags_ref, kv_ref, qg_hbm, far_ref, near_ref, out_ref,
    k_s, v_s, qg_ref, s_s, dp_s, dk_s, dv_s, sems
):
    sources, half = qg_ref.shape[0], near_ref.shape[0]
    rows = sources * DH
    copies = [pltpu.make_async_copy(qg_hbm, qg_ref, sems.at[0])]
    for kind, scratch in enumerate((k_s, v_s)):
        places = (
            (kv_ref.at[:, unit, kind], scratch.at[:sources]),
            (near_ref.at[:, kind], scratch.at[sources : sources + half]),
            (far_ref.at[:, kind], scratch.at[sources + half : sources + 2 * half]),
        )
        for i, (src, dst) in enumerate(places):
            copies.append(pltpu.make_async_copy(src, dst, sems.at[1 + 3 * kind + i]))
    for copy in copies:
        copy.start()
    dk_s[...] = jnp.zeros_like(dk_s)
    dv_s[...] = jnp.zeros_like(dv_s)
    for copy in copies:
        copy.wait()
    group, span = q_rows // DH, k_cols // DH

    def run(near, far):
        parts = list(range(0, sources, span))
        if near:
            parts += range(sources, sources + half, span)
        if far:
            parts += range(sources + half, sources + 2 * half, span)
        chunks = range(0, len(parts) * k_cols, k_cols)

        def part_of(scratch, c):
            i = parts[c // k_cols]
            return scratch[i : i + span].reshape(k_cols, DH)

        def block(i, carry):
            here = pl.ds(i * group, group)
            q = qg_ref[here, 0].reshape(q_rows, DH)
            g = qg_ref[here, 1].reshape(q_rows, DH)
            top = None
            for c in chunks:
                s = dot(q, part_of(k_s, c), NT)
                s_s[:, c : c + k_cols] = s
                part = fold(jnp.maximum, s)
                top = part if top is None else jnp.maximum(top, part)
            top = jnp.max(top, 1, keepdims=True) * SCALE2
            total = delta = out = None
            for c in chunks:
                e = jnp.exp2(s_s[:, c : c + k_cols] * SCALE2 - top)
                s_s[:, c : c + k_cols] = e
                dp = dot(g, part_of(v_s, c), NT)
                dp_s[:, c : c + k_cols] = dp
                t_part, d_part = fold(jnp.add, e), fold(jnp.add, e * dp)
                o_part = dot(e.astype(BF16), part_of(v_s, c), NN)
                total = t_part if total is None else total + t_part
                delta = d_part if delta is None else delta + d_part
                out = o_part if out is None else out + o_part
            inv = 1.0 / jnp.sum(total, 1, keepdims=True)
            delta = jnp.sum(delta, 1, keepdims=True) * inv
            out_ref[here, 0] = (out * inv).astype(BF16).reshape(group, DH, DH)
            g_over = (g.astype(F32) * inv).astype(BF16)
            q_over = (q.astype(F32) * (inv * SCALE)).astype(BF16)
            dq = None
            for c in chunks:
                e = s_s[:, c : c + k_cols]
                ds = (e * (dp_s[:, c : c + k_cols] - delta)).astype(BF16)
                part = dot(ds, part_of(k_s, c), NN)
                dq = part if dq is None else dq + part
                if c < rows:
                    dk_s[c : c + k_cols] += dot(ds, q_over, TN)
                    dv_s[c : c + k_cols] += dot(e.astype(BF16), g_over, TN)
            out_ref[here, 1] = (dq * (inv * SCALE)).astype(BF16).reshape(group, DH, DH)
            return carry

        lax.fori_loop(0, rows // q_rows, block, 0)

    for near in range(2):
        for far in range(2):
            here = (flags_ref[0] == near) & (flags_ref[1] == far)
            pl.when(here)(functools.partial(run, near, far))
    out_ref[:, 2] = dk_s[...].astype(BF16).reshape(rows // DH, DH, DH)
    out_ref[:, 3] = dv_s[...].astype(BF16).reshape(rows // DH, DH, DH)


def attention(flags, unit, kv, qg, near, far, q_rows=256, k_cols=1024):
    sources = qg.shape[0]
    rows, half = sources * DH, near.shape[0] * DH
    length = rows + 2 * half

    hbm = pl.BlockSpec(memory_space=pl.ANY)
    out = jax.ShapeDtypeStruct((sources, 4, DH, DH), BF16)
    return pl.pallas_call(
        functools.partial(attention_kernel, q_rows, k_cols, unit),
        grid=(1,),
        out_shape=out,
        in_specs=[pl.BlockSpec(memory_space=pltpu.SMEM), hbm, hbm, hbm, hbm],
        out_specs=pl.BlockSpec(out.shape, lambda i: (0, 0, 0, 0)),
        scratch_shapes=[
            pltpu.VMEM((length // DH, DH, DH), BF16),
            pltpu.VMEM((length // DH, DH, DH), BF16),
            pltpu.VMEM(qg.shape, BF16),
            pltpu.VMEM((q_rows, length), F32),
            pltpu.VMEM((q_rows, length), F32),
            pltpu.VMEM((rows, DH), F32),
            pltpu.VMEM((rows, DH), F32),
            pltpu.SemaphoreType.DMA((7,)),
        ],
        compiler_params=pltpu.CompilerParams(vmem_limit_bytes=ATTENTION_VMEM),
        cost_estimate=pl.CostEstimate(
            flops=40 * 10**9, bytes_accessed=6 * 2**20, transcendentals=rows * length
        ),
        name="attention",
    )(flags, kv, qg, far, near)


def column(dest, flip):
    head = dest + flip * (2 - dest % 4 // 2 * 4) if dest % 2 else dest
    return pl.ds(pl.multiple_of(head * DH, DH), DH)


def pack_kernel(count, flip_ref, *refs):
    for out_ref, pair in zip(refs[-count:], (refs[:2], refs[2:4])[:count]):
        for j in range(out_ref.shape[0]):
            for i, ref in enumerate(pair):
                out_ref[j, i] = ref[:, column(j, flip_ref[0])]


def pack_joint_kernel(flip_ref, x0_ref, y0_ref, x1_ref, y1_ref, out_ref):
    for unit, pair in enumerate(((x0_ref, y0_ref), (x1_ref, y1_ref))):
        for j in range(out_ref.shape[0]):
            for i, ref in enumerate(pair):
                out_ref[j, unit, i] = ref[:, column(j, flip_ref[0])]


def pack(flip, arrays, joint, step=8):
    tokens, width = arrays[0].shape
    dests = width // (2 * DH)
    steps = dests // step
    if joint:
        kernel, dims, count = pack_joint_kernel, (2, 2, tokens, DH), 1
    else:
        kernel, dims, count = functools.partial(pack_kernel, 2), (2, tokens, DH), 2
    spec = pl.BlockSpec((step, *dims), lambda j: (j,) + (0,) * len(dims))
    left = pl.BlockSpec((tokens, step * DH), lambda j: (0, j))
    right = pl.BlockSpec((tokens, step * DH), lambda j: (0, j + steps))
    return pl.pallas_call(
        kernel,
        grid=(steps,),
        out_shape=(jax.ShapeDtypeStruct((dests, *dims), BF16),) * count,
        in_specs=[pl.BlockSpec(memory_space=pltpu.SMEM), left, left, right, right],
        out_specs=[spec] * count,
        compiler_params=pltpu.CompilerParams(vmem_limit_bytes=56 * 2**20),
        cost_estimate=pl.CostEstimate(flops=0, bytes_accessed=4 * 2**20, transcendentals=0),
        name="pack",
    )(flip, *arrays, *arrays)


def unpack_kernel(step, flip_ref, x_ref, *refs):
    out_refs, (buf, sems) = refs[-6:-2], refs[-2:]
    i = pl.program_id(0)

    def fetch(n):
        return pltpu.make_async_copy(x_ref.at[pl.ds(n * step, step)], buf.at[n], sems.at[n])

    @pl.when(i == 0)
    def _():
        for n in range(buf.shape[0]):
            fetch(n).start()

    fetch(i).wait()
    for j in range(step):
        for kind, ref in enumerate(out_refs):
            ref[:, column(j, flip_ref[0])] = buf[i, j, kind]


def unpack(flip, unit, x, into=(), step=8):
    sources, _, tokens, _ = x.shape
    steps = sources // step
    shape = jax.ShapeDtypeStruct((tokens, sources * 2 * DH), BF16)
    return pl.pallas_call(
        functools.partial(unpack_kernel, step),
        grid=(steps,),
        out_shape=(shape,) * 4,
        in_specs=[
            pl.BlockSpec(memory_space=pltpu.SMEM),
            pl.BlockSpec(memory_space=pl.ANY),
        ]
        + [pl.BlockSpec(memory_space=pl.ANY)] * len(into),
        out_specs=[pl.BlockSpec((tokens, step * DH), lambda j: (0, j + unit * steps))] * 4,
        scratch_shapes=[
            pltpu.VMEM((steps, step, *x.shape[1:]), BF16),
            pltpu.SemaphoreType.DMA((steps,)),
        ],
        input_output_aliases={2 + i: i for i in range(len(into))},
        compiler_params=pltpu.CompilerParams(vmem_limit_bytes=COPY_VMEM),
        cost_estimate=pl.CostEstimate(flops=0, bytes_accessed=4 * 2**20, transcendentals=0),
        name="unpack",
    )(flip, x, *into)


def passed_along(block, distance):
    spans, width = lax.axis_size("span"), lax.axis_size("seq")
    route = []
    for c in range(spans - distance):
        crosses = (c < spans // 2) != (c + distance < spans // 2)
        for j in range(width):
            to = j ^ 2 if crosses and j % 2 else j
            route.append((c * width + j, (c + distance) * width + to))
    return lax.ppermute(block, ("span", "seq"), route)


def exchange(block):
    return lax.all_to_all(block, "seq", split_axis=0, concat_axis=0, tiled=True)


def body(queries, keys, values, out_grad, block_table):
    span = lax.axis_index("span")
    near = jnp.where(span >= 1, block_table[span, jnp.maximum(span - 1, 0)], 0) > 0
    far = jnp.where(span >= 2, block_table[span, jnp.maximum(span - 2, 0)], 0) > 0
    flags = jnp.stack([near, far]).astype(jnp.int32)
    flip = (span >= lax.axis_size("span") // 2).astype(jnp.int32)[None]
    kv = exchange(pack(flip, (keys, values), True)[0])
    packed = pack(flip, (queries, out_grad), False)
    tails = [kv[kv.shape[0] // 2 :, unit] for unit in range(2)]
    contexts = [(passed_along(t, 1), passed_along(t, 2)) for t in tails]
    results = ()
    for unit in range(2):
        y = attention(flags, unit, kv, exchange(packed[unit]), *contexts[unit])
        results = unpack(flip, unit, exchange(y), results)
    return tuple(results)


def solution(mesh):
    rows = P(("span", "seq"), None)
    return jax.shard_map(
        body,
        mesh=mesh,
        in_specs=(rows, rows, rows, rows, P()),
        out_specs=(rows, rows, rows, rows),
        check_vma=False,
    )
```
